32 devices in a mesh: grp: 8 (over z, x), rep: 4 (over y, core).
Axes of the slice: x: 2, y: 2, z: 4, core: 2. Of those that a mesh axis runs over, the one named last changes fastest.
Arguments:
- series: bfloat16 [256, 5632], P('grp'), may hold values from -6 to 6
- regressors: float32 [256, 24], P('grp'), may hold values from -3 to 3
- span_ids: int32 [256], replicated, may hold values from 0 to 3, never falling along the last dimension, each value on 1 to 128 neighbouring positions
- nuisance_count: int32 [1], replicated, may hold values from 12 to 24
- owner_order: int32 [8], replicated, may hold values from 0 to 7
- vectors: bfloat16 [5632, 64], P('grp'), may hold values from -0.3125 to 0.3125
Outputs:
- projected: float32 [5632, 64], P(('grp', 'rep'))
The draws below stay inside these ranges and needn't reach their ends.
Inputs may be any that keep to these rules, and one draw needn't show every extreme that they name: `span_ids`: never falls along frames; each of the 4 spans holds 1 to 128 frames, one exactly 128. `owner_order`: blocks may name the same slab.
All inputs are finite; a program needn't handle non-finite values.
Results may differ from the reference program's by a relative error of at most 0.0095.
Values may be sent and summed in bfloat16 or wider, within the bound.
A program may use at most 64 MiB of HBM per device.

```python
import math
import jax
import jax.numpy as jnp
import numpy as np
from jax import lax

FRAMES = 256
KMAX = 24
NVEC = 64
BLOCKS = 8
GROUPS = 8
SLAB = 704
GRAY = 5632
WINDOW = 5632


def nuisance_draw(key):
    nuis_key = jax.random.fold_in(key, 11)
    raw_draw = jax.random.normal(nuis_key, (FRAMES, KMAX), jnp.float32)
    return jnp.clip(raw_draw, -3.0, 3.0)


def draw_regressors(key, part):
    return nuisance_draw(key)


def draw_series(key, part):
    nuisance = nuisance_draw(key)
    subkeys = jax.random.split(jax.random.fold_in(key, 23), 5)
    networks = jax.random.randint(subkeys[0], (GRAY,), 0, 7)
    signals = jax.random.normal(subkeys[1], (FRAMES, 7), jnp.float32)
    picked = signals[:, networks]
    loading = jax.random.uniform(subkeys[2], (GRAY,), jnp.float32, 0.5, 1.5)
    noise_part = jax.random.normal(subkeys[3], (FRAMES, GRAY), jnp.float32)
    coupling = jnp.clip(jax.random.normal(subkeys[4], (6, GRAY), jnp.float32), -3.0, 3.0) * 0.8
    mixture = loading[None, :] * picked + noise_part
    loaded_columns = [0, 1, KMAX - 7, KMAX - 5, KMAX - 3, KMAX - 1]
    for position, column in enumerate(loaded_columns):
        mixture = mixture + nuisance[:, column][:, None] * coupling[position][None, :]
    return jnp.clip(mixture, -6.0, 6.0).astype(jnp.bfloat16)


def touch_ends(drawn, key, smallest, largest):
    longest = drawn.shape.index(max(drawn.shape))
    spots = []
    for shift in (0, 1):
        where = [jax.random.randint(jax.random.fold_in(key, axis), (), 0, length) for axis, length in enumerate(drawn.shape)]
        where[longest] = (where[longest] + shift) % drawn.shape[longest]
        spots.append(tuple(where))
    return drawn.at[spots[0]].set(smallest).at[spots[1]].set(largest)


def shard_levels(rng, shape, cuts, least, largest):
    def one(axis_at, shards_of):
        steps = jax.random.uniform(jax.random.fold_in(jax.random.fold_in(rng, 6), axis_at), (shards_of,), jnp.float32, least / len(cuts), largest / len(cuts))
        return jnp.repeat(jnp.exp(steps), shape[axis_at] // shards_of).reshape((-1,) + (1,) * (len(shape) - axis_at - 1))

    factor_of = one(*cuts[0])
    for cut in cuts[1:]:
        factor_of = factor_of * one(*cut)
    return factor_of


def length_profile(count, total, limit, slope):
    weights = [(1 << 20) // math.isqrt(grade ** slope) + 1 for grade in range(2, count + 1)]
    rest, given = total - limit - (count - 1), [1] * (count - 1)
    while rest > 0:
        movable = [i for i in range(count - 1) if given[i] < limit]
        whole, remaining = sum([weights[i] for i in movable]), rest
        for i in movable:
            more = min(limit - given[i], max(1, remaining * weights[i] // whole), rest)
            given[i] = given[i] + more
            rest = rest - more
    return np.array([limit] + given)


def uneven_parts(rng, number_of, total, reach, lean):
    if number_of == 2:
        one = jax.random.randint(rng, (), max(1, total - reach), min(reach, total - 1) + 1)
        return jnp.stack([one, total - one])
    sizes = jnp.asarray(length_profile(number_of, total, reach, lean), jnp.int32)
    twos = (number_of - 1) // 2
    giver, taker = sizes[1:1 + 2 * twos:2], sizes[2:2 + 2 * twos:2]
    room = jnp.minimum(giver - 1, reach - taker)
    moved = jax.random.randint(jax.random.fold_in(rng, 1), (twos,), 0, 1 << 20) % (room + 1)
    sizes = sizes.at[1:1 + 2 * twos:2].set(giver - moved).at[2:2 + 2 * twos:2].set(taker + moved)
    return sizes[jax.random.permutation(jax.random.fold_in(rng, 2), number_of)]


def scatter_about(own_key, extent, scale, limit, cuts=(), kind=jnp.bfloat16):
    entries = scale * jax.random.normal(own_key, extent, jnp.float32)
    if cuts:
        entries = entries * shard_levels(own_key, extent, cuts, -0.22, 0.18)
    return jnp.clip(entries, -limit, limit).astype(kind)


def setup_inputs(seed: int = 0) -> dict:
    key_list = jax.random.split(jax.random.key(seed), 7)
    return {
        "series": draw_series(jax.random.fold_in(key_list[6], 71), 0),
        "regressors": draw_regressors(jax.random.fold_in(key_list[6], 71), 0),
        "span_ids": jnp.searchsorted(jnp.cumsum(uneven_parts(key_list[2], 4, FRAMES, FRAMES // 2, 0)), jnp.arange(FRAMES), side="right").astype(jnp.int32),
        "nuisance_count": jax.random.randint(key_list[3], (1,), KMAX // 2, KMAX + 1).astype(jnp.int32),
        "owner_order": touch_ends(jax.random.randint(key_list[4], (BLOCKS,), 0, GROUPS), jax.random.fold_in(key_list[4], 1), 0, GROUPS - 1).astype(jnp.int32),
        "vectors": scatter_about(key_list[5], (GRAY, NVEC), (WINDOW // 16) ** -0.5, 0.3125, ((0, 8),)),
    }


fast_pole = 0.64
slow_pole = 0.955
corr_limit = 0.99
norm_eps = 1e-06

def fisher_map(correlation):
    clipped = jnp.clip(correlation, -corr_limit, corr_limit)
    return 0.5 * jnp.log((1.0 + clipped) / (1.0 - clipped))

def band_pass(columns_in, span_ids):
    continued = jnp.concatenate([jnp.zeros((1,), jnp.float32), (span_ids[1:] == span_ids[:-1]).astype(jnp.float32)])

    def advance(carried, inputs):
        fast_state, slow_state = carried
        sample, retain = inputs
        fast_state = fast_pole * retain * fast_state + (1.0 - fast_pole) * sample
        slow_state = slow_pole * retain * slow_state + (1.0 - slow_pole) * sample
        return ((fast_state, slow_state), fast_state - slow_state)
    initial = jnp.zeros((columns_in.shape[1],), jnp.float32)
    final_state, banded = lax.scan(advance, (initial, initial), (columns_in, continued))
    return banded

def solve_both(lower_factor, right_side):
    halfway = lax.linalg.triangular_solve(lower_factor, right_side, left_side=True, lower=True)
    return lax.linalg.triangular_solve(lower_factor, halfway, left_side=True, lower=True, transpose_a=True)

def reference(series, regressors, span_ids, nuisance_count, owner_order, vectors):
    highest = lax.Precision.HIGHEST
    filtered_series = band_pass(series.astype(jnp.float32), span_ids)
    filtered_nuisance = band_pass(regressors, span_ids)
    active = (jnp.arange(KMAX) < nuisance_count[0]).astype(jnp.float32)
    masked = filtered_nuisance * active[None, :]
    gram_matrix = jnp.dot(masked.T, masked, precision=highest) + jnp.diag(1.0 - active)
    lower_factor = jnp.linalg.cholesky(gram_matrix)
    coefficients = solve_both(lower_factor, jnp.dot(masked.T, filtered_series, precision=highest))
    cleaned = filtered_series - jnp.dot(masked, coefficients, precision=highest)
    centered = cleaned - lax.optimization_barrier(jnp.mean(cleaned, axis=0, keepdims=True))
    spread = lax.rsqrt(lax.optimization_barrier(jnp.mean(centered * centered, axis=0, keepdims=True)) + norm_eps)
    unit = (centered * spread * (1.0 / math.sqrt(FRAMES))).astype(jnp.bfloat16)
    projected = jnp.zeros((GRAY, NVEC), jnp.float32)
    for number in range(BLOCKS):
        first_col = (owner_order[number] * SLAB).astype(jnp.int32)
        window = lax.dynamic_slice_in_dim(unit, first_col, SLAB, 1)
        vec_rows = lax.dynamic_slice_in_dim(vectors, first_col, SLAB, 0)
        correlation = jnp.dot(unit.T.astype(jnp.float32), window.astype(jnp.float32), preferred_element_type=jnp.float32)
        fisher = fisher_map(correlation).astype(jnp.bfloat16)
        projected = projected + jnp.dot(fisher.astype(jnp.float32), vec_rows.astype(jnp.float32), preferred_element_type=jnp.float32)
    return projected
```

```python
import functools
import math

import jax
import jax.numpy as jnp
from jax import lax
from jax.experimental import pallas as pl
from jax.experimental.pallas import tpu as pltpu
from jax.sharding import PartitionSpec as P

BLOCKS = 8
MESH = pl.DeviceIdType.MESH
HIGHEST = lax.Precision.HIGHEST

fast_pole = 0.64
slow_pole = 0.955
corr_limit = 0.99
norm_eps = 1e-06


def dot32(a, b, ca, cb):
    return lax.dot_general(
        a, b, (((ca,), (cb,)), ((), ())), precision=HIGHEST, preferred_element_type=jnp.float32
    )


def dot16(a, b, ca, cb):
    return lax.dot_general(
        a, b, (((ca,), (cb,)), ((), ())), preferred_element_type=jnp.float32
    )


def band_matrix(span_row):
    frames = span_row.shape[1]
    across = jnp.broadcast_to(span_row.astype(jnp.float32), (frames, frames))
    down = across.T
    lag = lax.broadcasted_iota(jnp.int32, (frames, frames), 0) - lax.broadcasted_iota(
        jnp.int32, (frames, frames), 1
    )
    steps = jnp.maximum(lag, 0).astype(jnp.float32)
    fast = (1.0 - fast_pole) * jnp.exp(steps * math.log(fast_pole))
    slow = (1.0 - slow_pole) * jnp.exp(steps * math.log(slow_pole))
    return jnp.where((lag >= 0) & (across == down), fast - slow, 0.0)


def spd_inverse(gram):
    size = gram.shape[0]
    lane = lax.broadcasted_iota(jnp.int32, (size, size), 1)
    sub = lax.broadcasted_iota(jnp.int32, (size, size), 0)

    def sweep(k, m):
        on_col, on_row = lane == k, sub == k
        col = jnp.sum(jnp.where(on_col, m, 0.0), axis=1, keepdims=True)
        row = jnp.sum(jnp.where(on_row, m, 0.0), axis=0, keepdims=True)
        pivot = jnp.sum(jnp.where(on_col & on_row, m, 0.0), axis=(0, 1), keepdims=True)
        inv = 1.0 / pivot
        rest = m - col * (row * inv)
        return jnp.where(
            on_row,
            jnp.where(on_col, inv, row * inv),
            jnp.where(on_col, -col * inv, rest),
        )

    return lax.fori_loop(0, size, sweep, gram)


def kernel(
    series, regs, span, count, owner, vectors, out,
    win, rows, nreg, vto, vtb, vtf, a_hi, a_lo, unit_rows, parts, other,
    send, reg_r, win_r, core_r, vt_r, vtc_r, rows_r, fin_r, loc,
):
    grp, rep = lax.axis_index("grp"), lax.axis_index("rep")
    z, x = grp // 2, grp % 2
    y, c = rep // 2, rep % 2
    groups = lax.axis_size("grp")
    nz = groups // 2
    frames_loc, gray = series.shape
    half = gray // 2
    piece = half // 2
    slab = gray // groups
    wide = rows.shape[1]
    per_half = groups // 2
    quarter = out.shape[0]
    home = z // (nz // 2) == y
    away = z // (nz // 2) != y
    mine = grp % per_half

    def at(zz, xx, yy, cc):
        return (zz * 2 + xx, yy * 2 + cc)

    zs = [lax.rem(z + d, nz) for d in range(1, nz)]
    x_peer = at(z, 1 - x, y, c)
    core_peer = at(z, x, y, 1 - c)
    y_peer = at(z, x, 1 - y, c)

    barrier = pltpu.get_barrier_semaphore()
    everyone = [at(zz, x, y, c) for zz in zs] + [x_peer, core_peer, y_peer]
    for peer in everyone:
        pl.semaphore_signal(barrier, inc=1, device_id=peer, device_id_type=MESH)

    sent = []
    counter = [0]

    def push(src, dst, recv, peer, cond=None):
        k = counter[0]
        counter[0] += 1
        copy = pltpu.make_async_remote_copy(
            src_ref=src, dst_ref=dst, send_sem=send.at[k], recv_sem=recv,
            device_id=peer, device_id_type=MESH,
        )
        if cond is None:
            copy.start()
        else:
            pl.when(cond)(copy.start)
        sent.append((copy, cond))

    def arrive(dst, recv):
        pltpu.make_async_copy(dst, dst, recv).wait()

    def rows_of(s):
        return pl.ds(pl.multiple_of(s * frames_loc, frames_loc), frames_loc)

    own_cols = pl.ds(pl.multiple_of(c * piece, 128), piece)
    core_cols = pl.ds(pl.multiple_of((1 - c) * piece, 128), piece)
    series_cols = pl.ds(pl.multiple_of(y * half + c * piece, 128), piece)
    slab_at = pl.multiple_of(grp * slab - (slab % 128) * x, 128)
    slab_in_half = pl.multiple_of(mine * slab - (slab % 128) * x, 128)
    vt_half = pl.ds(pl.multiple_of(c * 32, 32), 32)
    vt_other = pl.ds(pl.multiple_of((1 - c) * 32, 32), 32)

    local_win = pltpu.make_async_copy(
        series.at[:, pl.ds(pl.multiple_of(y * half, 128), half)], win.at[rows_of(grp), :], loc.at[0]
    )
    local_rows = pltpu.make_async_copy(
        series.at[:, pl.ds(slab_at, wide)], rows.at[rows_of(grp), :], loc.at[1]
    )
    local_win.start()
    local_rows.start()
    nreg[rows_of(grp), :] = regs[...]
    nvec = vectors.shape[1]
    eye = (
        lax.broadcasted_iota(jnp.int32, (nvec, nvec), 0)
        == lax.broadcasted_iota(jnp.int32, (nvec, nvec), 1)
    ).astype(jnp.float32).astype(jnp.bfloat16)
    vto[...] = dot16(eye, vectors[...], 1, 1).astype(jnp.bfloat16)

    @pl.when(home)
    def _():
        vtb[mine] = vto[...]

    pl.semaphore_wait(barrier, len(everyone))

    for zz in zs + [None]:
        peer = x_peer if zz is None else at(zz, x, y, c)
        push(regs, nreg.at[rows_of(grp), :], reg_r.at[grp], peer)
    for zz in zs + [None]:
        peer = x_peer if zz is None else at(zz, x, y, c)
        push(series.at[:, series_cols], win.at[rows_of(grp), own_cols], win_r.at[grp], peer)
    for zz in zs + [None]:
        peer = x_peer if zz is None else at(zz, x, y, c)
        push(vto.at[vt_half, :], vtb.at[mine, vt_half, :], vt_r.at[mine], peer, home)

    filt = band_matrix(span[...])

    back = [lax.rem(z + nz - d, nz) for d in range(1, nz)]
    for zz in back:
        s = zz * 2 + x
        arrive(nreg.at[rows_of(s), :], reg_r.at[s])
        push(nreg.at[rows_of(s), :], nreg.at[rows_of(s), :], reg_r.at[s], x_peer)

    def from_z(zz):
        s = zz * 2 + x
        here = win.at[rows_of(s), own_cols]
        arrive(here, win_r.at[s])
        push(here, here, win_r.at[s], x_peer)
        push(here, here, core_r.at[s], core_peer)

    from_z(back[0])

    for zz in [z] + back:
        s = zz * 2 + 1 - x
        arrive(nreg.at[rows_of(s), :], reg_r.at[s])

    kmax = regs.shape[1]
    active = (lax.broadcasted_iota(jnp.int32, (1, kmax), 1) < count[0]).astype(jnp.float32)
    masked = dot32(filt, nreg[...], 1, 0) * active
    diag = (
        lax.broadcasted_iota(jnp.int32, (kmax, kmax), 0)
        == lax.broadcasted_iota(jnp.int32, (kmax, kmax), 1)
    )
    gram = dot32(masked, masked, 0, 0) + jnp.where(diag, 1.0 - active, 0.0)
    inverse = spd_inverse(gram)

    for zz in back[1:]:
        from_z(zz)

    for zz in back:
        s = zz * 2 + x
        t = lax.rem(s, per_half)
        want = zz // (nz // 2) == y
        here = vtb.at[t, vt_half, :]

        def took(here=here, t=t):
            arrive(here, vt_r.at[t])

        pl.when(want)(took)
        push(here, here, vt_r.at[t], x_peer, want)
        push(here, here, vtc_r.at[t], core_peer, want)

    fitted = dot32(inverse, dot32(masked, filt, 0, 0), 1, 0)
    clean = filt - dot32(masked, fitted, 1, 0)
    clean = clean - jnp.mean(clean, axis=0, keepdims=True)
    hi = clean.astype(jnp.bfloat16)
    a_hi[...] = hi
    a_lo[...] = (clean - hi.astype(jnp.float32)).astype(jnp.bfloat16)

    for zz in [z] + back:
        s = zz * 2 + 1 - x
        here = win.at[rows_of(s), own_cols]
        arrive(here, win_r.at[s])
        push(here, here, core_r.at[s], core_peer)

    for zz in [z] + back:
        s = zz * 2 + 1 - x
        t = lax.rem(s, per_half)
        want = zz // (nz // 2) == y
        here = vtb.at[t, vt_half, :]

        def took(here=here, t=t):
            arrive(here, vt_r.at[t])

        pl.when(want)(took)
        push(here, here, vtc_r.at[t], core_peer, want)

    order = [zz * 2 + x for zz in back] + [zz * 2 + 1 - x for zz in [z] + back]
    inner = []
    for n, s in enumerate(order):
        arrive(win.at[rows_of(s), core_cols], core_r.at[s])
        src = win.at[rows_of(s), pl.ds(slab_in_half, wide)]
        push(src, rows.at[rows_of(s), :], rows_r.at[s], y_peer, home)
        keep = pltpu.make_async_copy(src, rows.at[rows_of(s), :], loc.at[2 + n])
        pl.when(home)(keep.start)
        inner.append(keep)

    local_win.wait()
    local_rows.wait()

    for xx, list_z in ((x, back), (1 - x, [z] + back)):
        for zz in list_z:
            t = lax.rem(zz * 2 + xx, per_half)
            want = zz // (nz // 2) == y

            def took(t=t):
                arrive(vtb.at[t, vt_other, :], vtc_r.at[t])

            pl.when(want)(took)
    vtf[...] = jnp.concatenate([vtb[t] for t in range(per_half)], axis=1)

    def normal(block):
        centered = dot16(a_hi[...], block, 1, 0) + dot16(a_lo[...], block, 1, 0)
        power = jnp.mean(centered * centered, axis=0, keepdims=True) + norm_eps
        return centered * (lax.rsqrt(power) * (1.0 / math.sqrt(centered.shape[0])))

    for n, s in enumerate(order):
        def wait_away(s=s):
            arrive(rows.at[rows_of(s), :], rows_r.at[s])

        pl.when(away)(wait_away)
        pl.when(home)(inner[n].wait)
    unit_rows[...] = normal(rows[...]).T.astype(jnp.bfloat16)
    first = (slab % 128) * x + quarter * c
    left = jnp.concatenate(
        [
            unit_rows[pl.ds(pl.multiple_of(first + 2 * quarter * k, 16), quarter), :]
            for k in range(2)
        ],
        axis=0,
    )

    width = 256
    lane = lax.broadcasted_iota(jnp.int32, (1, width), 1)

    def fold(j, total):
        cols = pl.ds(pl.multiple_of(j * width, width), width)
        unit = normal(win[:, cols]).astype(jnp.bfloat16)
        corr = jnp.clip(dot16(left, unit, 1, 0), -corr_limit, corr_limit)
        place = lane + j * width
        which = jnp.full((1, width), y * per_half, jnp.int32)
        for t in range(1, per_half):
            which = which + (place >= t * slab).astype(jnp.int32)
        times = jnp.zeros((1, width), jnp.float32)
        for b in range(BLOCKS):
            times = times + jnp.where(which == owner[b], 0.5, 0.0)
        fisher = ((jnp.log(1.0 + corr) - jnp.log(1.0 - corr)) * times).astype(jnp.bfloat16)
        return total + dot16(fisher, vtf[:, cols], 1, 1)

    total = lax.fori_loop(
        0, half // width, fold, jnp.zeros((2 * quarter, nvec), jnp.float32)
    )
    parts[0] = total[:quarter]
    parts[1] = total[quarter:]
    push(parts.at[1 - y], other, fin_r, y_peer)
    arrive(other, fin_r)
    out[...] = parts[y] + other[...]
    for copy, cond in sent:
        if cond is None:
            copy.wait_send()
        else:
            pl.when(cond)(copy.wait_send)


def one_kernel(series, regressors, span_ids, nuisance_count, owner_order, vectors):
    groups, reps = lax.axis_size("grp"), lax.axis_size("rep")
    frames_loc, gray = series.shape
    frames = frames_loc * groups
    slab = gray // groups
    quarter = slab // reps
    wide = -(-slab // 128) * 128
    nvec = vectors.shape[1]
    vm = pl.BlockSpec(memory_space=pltpu.VMEM)
    sm = pl.BlockSpec(memory_space=pltpu.SMEM)
    dma = pltpu.SemaphoreType.DMA
    return pl.pallas_call(
        kernel,
        out_shape=jax.ShapeDtypeStruct((quarter, nvec), jnp.float32),
        in_specs=[pl.BlockSpec(memory_space=pl.ANY), vm, vm, sm, sm, vm],
        out_specs=vm,
        scratch_shapes=[
            pltpu.VMEM((frames, gray // 2), jnp.bfloat16),
            pltpu.VMEM((frames, wide), jnp.bfloat16),
            pltpu.VMEM((frames, regressors.shape[1]), jnp.float32),
            pltpu.VMEM((nvec, slab), jnp.bfloat16),
            pltpu.VMEM((groups // 2, nvec, slab), jnp.bfloat16),
            pltpu.VMEM((nvec, gray // 2), jnp.bfloat16),
            pltpu.VMEM((frames, frames), jnp.bfloat16),
            pltpu.VMEM((frames, frames), jnp.bfloat16),
            pltpu.VMEM((wide, frames), jnp.bfloat16),
            pltpu.VMEM((2, quarter, nvec), jnp.float32),
            pltpu.VMEM((quarter, nvec), jnp.float32),
            dma((64,)),
            dma((groups,)), dma((groups,)), dma((groups,)),
            dma((groups // 2,)), dma((groups // 2,)),
            dma((groups,)), dma, dma((16,)),
        ],
        compiler_params=pltpu.CompilerParams(
            collective_id=0, has_side_effects=True, vmem_limit_bytes=40 * 1024 * 1024
        ),
    )(series, regressors, span_ids[None, :], nuisance_count, owner_order, vectors)


def spread_2(value, axis, root):
    mine = lax.axis_index(axis) == root
    return lax.psum(jnp.where(mine, value, jnp.zeros_like(value)), axis)


def fisher_map(correlation):
    clipped = jnp.clip(correlation, -corr_limit, corr_limit)
    return 0.5 * jnp.log((1.0 + clipped) / (1.0 - clipped))


def block_operators(span_ids, frames):
    offsets = jnp.arange(128)
    lag_steps = offsets[:, None] - offsets[None, :]
    lag_clip = jnp.maximum(lag_steps, 0).astype(jnp.float32)
    operators = []
    for number in range(frames // 128):
        ids_here = span_ids[number * 128 : (number + 1) * 128]
        joined = (ids_here[:, None] == ids_here[None, :]) & (lag_steps >= 0)
        if number == 0:
            linked = jnp.zeros((128,), jnp.float32)
        else:
            linked = (ids_here == span_ids[number * 128 - 1]).astype(jnp.float32)
        pole_pair = []
        for pole_value in (fast_pole, slow_pole):
            matrix = jnp.where(
                joined, (1.0 - pole_value) * jnp.exp(lag_clip * math.log(pole_value)), 0.0
            )
            carried = linked * jnp.exp((offsets + 1).astype(jnp.float32) * math.log(pole_value))
            pole_pair.append((matrix, carried))
        operators.append(pole_pair)
    return operators


def band_pass(columns_in, operators):
    col_count = columns_in.shape[1]
    states = [jnp.zeros((col_count,), jnp.float32), jnp.zeros((col_count,), jnp.float32)]
    pieces = []
    for number, pole_pair in enumerate(operators):
        segment = columns_in[number * 128 : (number + 1) * 128]
        outputs = []
        for pole_slot in range(2):
            matrix, carried = pole_pair[pole_slot]
            response = (
                jnp.dot(matrix, segment, precision=lax.Precision.HIGHEST)
                + carried[:, None] * states[pole_slot][None, :]
            )
            states[pole_slot] = response[-1]
            outputs.append(response)
        pieces.append(outputs[0] - outputs[1])
    return jnp.concatenate(pieces, axis=0)


def nuisance_basis(filtered_nuisance, nuisance_count):
    active = (jnp.arange(filtered_nuisance.shape[1]) < nuisance_count[0]).astype(jnp.float32)
    masked = filtered_nuisance * active[None, :]
    gram_matrix = jnp.dot(masked.T, masked, precision=lax.Precision.HIGHEST) + jnp.diag(
        1.0 - active
    )
    return (masked, jnp.linalg.cholesky(gram_matrix))


def scale_columns(filtered, masked, lower_factor):
    highest = lax.Precision.HIGHEST
    right_side = jnp.dot(masked.T, filtered, precision=highest)
    halfway = lax.linalg.triangular_solve(lower_factor, right_side, left_side=True, lower=True)
    coefficients = lax.linalg.triangular_solve(
        lower_factor, halfway, left_side=True, lower=True, transpose_a=True
    )
    cleaned = filtered - jnp.dot(masked, coefficients, precision=highest)
    centered = cleaned - jnp.mean(cleaned, axis=0, keepdims=True)
    spread = lax.rsqrt(jnp.mean(centered * centered, axis=0, keepdims=True) + norm_eps)
    return (centered * spread * (1.0 / math.sqrt(centered.shape[0]))).astype(jnp.bfloat16)


def fold_tile(my_cols, vec_slab, running, part_cols):
    correlation = lax.dot_general(
        my_cols, part_cols, (((0,), (0,)), ((), ())), preferred_element_type=jnp.float32
    )
    fisher = fisher_map(correlation).astype(jnp.bfloat16)
    return running + jnp.dot(fisher, vec_slab, preferred_element_type=jnp.float32)


def by_block(series, regressors, span_ids, nuisance_count, owner_order, vectors):
    grp_count = lax.axis_size("grp")
    rep_count = lax.axis_size("rep")
    rep_index = lax.axis_index("rep")
    frames_loc = series.shape[0]
    frames = frames_loc * grp_count
    own_cols = series.shape[1] // (grp_count * rep_count)
    operators = block_operators(span_ids, frames)
    nuisance = lax.all_gather(regressors, "grp", axis=0, tiled=True)
    masked, lower_factor = nuisance_basis(band_pass(nuisance, operators), nuisance_count)
    quarter = series.reshape(frames_loc, grp_count, rep_count, own_cols)
    quarter = lax.dynamic_slice_in_dim(quarter, rep_index, 1, 2).reshape(
        frames_loc, grp_count, own_cols
    )
    filtered = band_pass(
        lax.all_to_all(quarter, "grp", split_axis=1, concat_axis=0, tiled=True)[:, 0, :].astype(
            jnp.float32
        ),
        operators,
    )
    unit_cols = scale_columns(filtered, masked, lower_factor)
    projected = jnp.zeros((own_cols, vectors.shape[1]), jnp.float32)
    for number in range(BLOCKS):
        piece_in, vec_slab = (
            spread_2(unit_cols, "grp", owner_order[number]),
            spread_2(vectors, "grp", owner_order[number]),
        )
        projected = fold_tile(
            unit_cols, vec_slab, projected, lax.all_gather(piece_in, "rep", axis=1, tiled=True)
        )
    return projected


def solution(mesh):
    local = one_kernel if mesh.shape["grp"] <= BLOCKS else by_block
    placed = (P("grp", None), P("grp", None), P(), P(), P(), P("grp", None))
    return jax.shard_map(
        local, mesh=mesh, in_specs=placed, out_specs=P(("grp", "rep"), None), check_vma=False
    )
```

```python
import functools
import math

import jax
import jax.numpy as jnp
from jax import lax
from jax.experimental import pallas as pl
from jax.experimental.pallas import tpu as pltpu
from jax.sharding import PartitionSpec as P

BLOCKS = 8
MESH = pl.DeviceIdType.MESH
HIGHEST = lax.Precision.HIGHEST

fast_pole = 0.64
slow_pole = 0.955
corr_limit = 0.99
norm_eps = 1e-06


def dot32(a, b, ca, cb):
    return lax.dot_general(
        a, b, (((ca,), (cb,)), ((), ())), precision=HIGHEST, preferred_element_type=jnp.float32
    )


def dot16(a, b, ca, cb):
    return lax.dot_general(
        a, b, (((ca,), (cb,)), ((), ())), preferred_element_type=jnp.float32
    )


def band_matrix(span_row):
    frames = span_row.shape[1]
    across = jnp.broadcast_to(span_row.astype(jnp.float32), (frames, frames))
    down = across.T
    lag = lax.broadcasted_iota(jnp.int32, (frames, frames), 0) - lax.broadcasted_iota(
        jnp.int32, (frames, frames), 1
    )
    steps = jnp.maximum(lag, 0).astype(jnp.float32)
    fast = (1.0 - fast_pole) * jnp.exp(steps * math.log(fast_pole))
    slow = (1.0 - slow_pole) * jnp.exp(steps * math.log(slow_pole))
    return jnp.where((lag >= 0) & (across == down), fast - slow, 0.0)


def spd_inverse(gram):
    size = gram.shape[0]
    lane = lax.broadcasted_iota(jnp.int32, (size, size), 1)
    sub = lax.broadcasted_iota(jnp.int32, (size, size), 0)

    def sweep(k, m):
        on_col, on_row = lane == k, sub == k
        col = jnp.sum(jnp.where(on_col, m, 0.0), axis=1, keepdims=True)
        row = jnp.sum(jnp.where(on_row, m, 0.0), axis=0, keepdims=True)
        pivot = jnp.sum(jnp.where(on_col & on_row, m, 0.0), axis=(0, 1), keepdims=True)
        inv = 1.0 / pivot
        rest = m - col * (row * inv)
        return jnp.where(
            on_row,
            jnp.where(on_col, inv, row * inv),
            jnp.where(on_col, -col * inv, rest),
        )

    return lax.fori_loop(0, size, sweep, gram)


def kernel(
    series, regs, span, count, owner, vectors, out,
    win, rows, nreg, vtb, a_hi, a_lo, unit, unit_rows, parts, other,
    send, reg_r, win_r, vt_r, rows_r, fin_r, loc,
):
    grp, rep = lax.axis_index("grp"), lax.axis_index("rep")
    z, x = grp // 2, grp % 2
    y, c = rep // 2, rep % 2
    groups = lax.axis_size("grp")
    reps = lax.axis_size("rep")
    nz = groups // 2
    frames_loc, gray = series.shape
    slab = gray // groups
    part = 2 * slab
    wide = rows.shape[1]
    quarter = out.shape[1]
    pair = y + c * (nz - 1 - 2 * y)
    home = pair == z
    away = pair != z

    near = z + 1 - 2 * (z % 2)
    far = [nz - 1 - z, lax.rem(z + nz // 2, nz)]
    lines = [near] + far
    x_peer = (z * 2 + 1 - x, rep)
    diagonal = (near * 2 + 1 - x, rep)
    direct = [(zz * 2 + x, rep) for zz in lines] + [x_peer, diagonal]
    mates = [lax.rem(rep + d, reps) for d in range(1, reps)]

    barrier = pltpu.get_barrier_semaphore()
    everyone = direct + [(grp, k) for k in mates]
    for peer in everyone:
        pl.semaphore_signal(barrier, inc=1, device_id=peer, device_id_type=MESH)

    sent = []

    def push(src, dst, recv, peer, cond=None):
        copy = pltpu.make_async_remote_copy(
            src_ref=src, dst_ref=dst, send_sem=send.at[len(sent)], recv_sem=recv,
            device_id=peer, device_id_type=MESH,
        )
        if cond is None:
            copy.start()
        else:
            pl.when(cond)(copy.start)
        sent.append((copy, cond))

    def arrive(dst, recv):
        pltpu.make_async_copy(dst, dst, recv).wait()

    def rows_of(s):
        return pl.ds(pl.multiple_of(s * frames_loc, frames_loc), frames_loc)

    part_cols = pl.ds(pl.multiple_of(pair * part, 128), part)
    slab_at = pl.multiple_of(grp * slab - (slab % 128) * x, 128)
    slab_in_part = pl.ds(pl.multiple_of(x * (slab - slab % 128), 128), wide)

    local_win = pltpu.make_async_copy(
        series.at[:, part_cols], win.at[rows_of(grp), :], loc.at[0]
    )
    local_rows = pltpu.make_async_copy(
        series.at[:, pl.ds(slab_at, wide)], rows.at[rows_of(grp), :], loc.at[1]
    )
    local_win.start()
    local_rows.start()
    nreg[grp] = regs[...]
    nvec = vectors.shape[0]

    @pl.when(home)
    def _():
        vtb[x] = vectors[...]

    pl.semaphore_wait(barrier, len(everyone))

    for peer in direct:
        push(regs, nreg.at[grp], reg_r.at[grp], peer)
    for peer in direct:
        push(series.at[:, part_cols], win.at[rows_of(grp), :], win_r.at[grp], peer)
    for peer in direct:
        push(vectors, vtb.at[x], vt_r.at[x], peer, home)

    filt = band_matrix(span[...])

    for zz in far:
        s = zz * 2 + x
        arrive(nreg.at[s], reg_r.at[s])
        push(nreg.at[s], nreg.at[s], reg_r.at[s], x_peer)
    for s in [near * 2 + x] + [zz * 2 + 1 - x for zz in [z, near] + far]:
        arrive(nreg.at[s], reg_r.at[s])

    kmax = regs.shape[0]
    active = (lax.broadcasted_iota(jnp.int32, (kmax, 1), 0) < count[0]).astype(jnp.float32)
    frames_in = jnp.concatenate([nreg[s] for s in range(groups)], axis=1)
    masked = dot32(frames_in, filt, 1, 1) * active
    diag = (
        lax.broadcasted_iota(jnp.int32, (kmax, kmax), 0)
        == lax.broadcasted_iota(jnp.int32, (kmax, kmax), 1)
    )
    gram = dot32(masked, masked, 1, 1) + jnp.where(diag, 1.0 - active, 0.0)
    inverse = spd_inverse(gram)

    keeps = []

    def landed(s, forward):
        here = win.at[rows_of(s), :]
        arrive(here, win_r.at[s])
        if forward:
            push(here, here, win_r.at[s], x_peer)
        src = win.at[rows_of(s), slab_in_part]
        dst = rows.at[rows_of(s), :]
        for k in mates:
            push(src, dst, rows_r.at[s], (grp, k), home)
        keep = pltpu.make_async_copy(src, dst, loc.at[2 + len(keeps)])
        pl.when(home)(keep.start)
        keeps.append((keep, dst, rows_r.at[s]))

    for zz in far:
        landed(zz * 2 + x, True)
    landed(near * 2 + x, False)
    landed(z * 2 + 1 - x, False)
    landed(near * 2 + 1 - x, False)

    fitted = dot32(inverse, dot32(masked, filt, 1, 0), 1, 0)
    clean = filt - dot32(masked, fitted, 0, 0)
    clean = clean - jnp.mean(clean, axis=0, keepdims=True)
    hi = clean.astype(jnp.bfloat16)
    a_hi[...] = hi
    a_lo[...] = (clean - hi.astype(jnp.float32)).astype(jnp.bfloat16)

    pl.when(away)(lambda: arrive(vtb.at[x], vt_r.at[x]))
    push(vtb.at[x], vtb.at[x], vt_r.at[x], x_peer, (pair != z) & (pair != near))

    for zz in far:
        landed(zz * 2 + 1 - x, False)
    local_win.wait()
    local_rows.wait()

    def normal(block):
        centered = dot16(a_hi[...], block, 1, 0) + dot16(a_lo[...], block, 1, 0)
        power = jnp.mean(centered * centered, axis=0, keepdims=True) + norm_eps
        return centered * (lax.rsqrt(power) * (1.0 / math.sqrt(centered.shape[0])))

    for start in range(0, part, 256):
        cols = slice(start, min(start + 256, part))
        unit[:, cols] = normal(win[:, cols]).astype(jnp.bfloat16)

    arrive(vtb.at[1 - x], vt_r.at[1 - x])
    right = jnp.concatenate([vtb[t] for t in range(2)], axis=1)
    place = lax.broadcasted_iota(jnp.int32, (1, part), 1)
    which = 2 * pair + (place >= slab).astype(jnp.int32)
    times = jnp.zeros((1, part), jnp.float32)
    for b in range(BLOCKS):
        times = times + jnp.where(which == owner[b], 0.5, 0.0)

    for keep, dst, recv in keeps:
        pl.when(away)(functools.partial(arrive, dst, recv))
        pl.when(home)(keep.wait)
    for start in range(0, wide, 256):
        cols = slice(start, start + 256)
        unit_rows[cols, :] = normal(rows[:, cols]).T.astype(jnp.bfloat16)

    for k in mates + [rep]:
        first = pl.multiple_of((slab % 128) * x + quarter * k, 16)
        left = unit_rows[pl.ds(first, quarter), :]
        corr = jnp.clip(dot16(left, unit[...], 1, 0), -corr_limit, corr_limit)
        fisher = ((jnp.log(1.0 + corr) - jnp.log(1.0 - corr)) * times).astype(jnp.bfloat16)
        parts[k] = dot16(right, fisher, 1, 1)
        if k is not rep:
            push(parts.at[k], other.at[rep], fin_r.at[rep], (grp, k))
    total = parts[rep]
    for k in mates:
        arrive(other.at[k], fin_r.at[k])
        total = total + other[k]
    out[...] = total
    for copy, cond in sent:
        if cond is None:
            copy.wait_send()
        else:
            pl.when(cond)(copy.wait_send)


def one_kernel(series, regressors, span_ids, nuisance_count, owner_order, vectors):
    groups, reps = lax.axis_size("grp"), lax.axis_size("rep")
    frames_loc, gray = series.shape
    frames = frames_loc * groups
    slab = gray // groups
    quarter = slab // reps
    wide = -(-slab // 128) * 128
    nvec = vectors.shape[1]
    vm = pl.BlockSpec(memory_space=pltpu.VMEM)
    sm = pl.BlockSpec(memory_space=pltpu.SMEM)
    dma = pltpu.SemaphoreType.DMA
    return pl.pallas_call(
        kernel,
        out_shape=jax.ShapeDtypeStruct((nvec, quarter), jnp.float32),
        in_specs=[pl.BlockSpec(memory_space=pl.ANY), vm, vm, sm, sm, vm],
        out_specs=vm,
        scratch_shapes=[
            pltpu.VMEM((frames, 2 * slab), jnp.bfloat16),
            pltpu.VMEM((frames, wide), jnp.bfloat16),
            pltpu.VMEM((groups, regressors.shape[1], frames_loc), jnp.float32),
            pltpu.VMEM((2, nvec, slab), jnp.bfloat16),
            pltpu.VMEM((frames, frames), jnp.bfloat16),
            pltpu.VMEM((frames, frames), jnp.bfloat16),
            pltpu.VMEM((frames, 2 * slab), jnp.bfloat16),
            pltpu.VMEM((wide, frames), jnp.bfloat16),
            pltpu.VMEM((reps, nvec, quarter), jnp.float32),
            pltpu.VMEM((reps, nvec, quarter), jnp.float32),
            dma((64,)),
            dma((groups,)), dma((groups,)), dma((2,)),
            dma((groups,)), dma((reps,)), dma((16,)),
        ],
        compiler_params=pltpu.CompilerParams(
            collective_id=0, has_side_effects=True, vmem_limit_bytes=60 * 1024 * 1024
        ),
    )(series, regressors.T, span_ids[None, :], nuisance_count, owner_order, vectors.T).T


def spread_2(value, axis, root):
    mine = lax.axis_index(axis) == root
    return lax.psum(jnp.where(mine, value, jnp.zeros_like(value)), axis)


def fisher_map(correlation):
    clipped = jnp.clip(correlation, -corr_limit, corr_limit)
    return 0.5 * jnp.log((1.0 + clipped) / (1.0 - clipped))


def block_operators(span_ids, frames):
    offsets = jnp.arange(128)
    lag_steps = offsets[:, None] - offsets[None, :]
    lag_clip = jnp.maximum(lag_steps, 0).astype(jnp.float32)
    operators = []
    for number in range(frames // 128):
        ids_here = span_ids[number * 128 : (number + 1) * 128]
        joined = (ids_here[:, None] == ids_here[None, :]) & (lag_steps >= 0)
        if number == 0:
            linked = jnp.zeros((128,), jnp.float32)
        else:
            linked = (ids_here == span_ids[number * 128 - 1]).astype(jnp.float32)
        pole_pair = []
        for pole_value in (fast_pole, slow_pole):
            matrix = jnp.where(
                joined, (1.0 - pole_value) * jnp.exp(lag_clip * math.log(pole_value)), 0.0
            )
            carried = linked * jnp.exp((offsets + 1).astype(jnp.float32) * math.log(pole_value))
            pole_pair.append((matrix, carried))
        operators.append(pole_pair)
    return operators


def band_pass(columns_in, operators):
    col_count = columns_in.shape[1]
    states = [jnp.zeros((col_count,), jnp.float32), jnp.zeros((col_count,), jnp.float32)]
    pieces = []
    for number, pole_pair in enumerate(operators):
        segment = columns_in[number * 128 : (number + 1) * 128]
        outputs = []
        for pole_slot in range(2):
            matrix, carried = pole_pair[pole_slot]
            response = (
                jnp.dot(matrix, segment, precision=lax.Precision.HIGHEST)
                + carried[:, None] * states[pole_slot][None, :]
            )
            states[pole_slot] = response[-1]
            outputs.append(response)
        pieces.append(outputs[0] - outputs[1])
    return jnp.concatenate(pieces, axis=0)


def nuisance_basis(filtered_nuisance, nuisance_count):
    active = (jnp.arange(filtered_nuisance.shape[1]) < nuisance_count[0]).astype(jnp.float32)
    masked = filtered_nuisance * active[None, :]
    gram_matrix = jnp.dot(masked.T, masked, precision=lax.Precision.HIGHEST) + jnp.diag(
        1.0 - active
    )
    return (masked, jnp.linalg.cholesky(gram_matrix))


def scale_columns(filtered, masked, lower_factor):
    highest = lax.Precision.HIGHEST
    right_side = jnp.dot(masked.T, filtered, precision=highest)
    halfway = lax.linalg.triangular_solve(lower_factor, right_side, left_side=True, lower=True)
    coefficients = lax.linalg.triangular_solve(
        lower_factor, halfway, left_side=True, lower=True, transpose_a=True
    )
    cleaned = filtered - jnp.dot(masked, coefficients, precision=highest)
    centered = cleaned - jnp.mean(cleaned, axis=0, keepdims=True)
    spread = lax.rsqrt(jnp.mean(centered * centered, axis=0, keepdims=True) + norm_eps)
    return (centered * spread * (1.0 / math.sqrt(centered.shape[0]))).astype(jnp.bfloat16)


def fold_tile(my_cols, vec_slab, running, part_cols):
    correlation = lax.dot_general(
        my_cols, part_cols, (((0,), (0,)), ((), ())), preferred_element_type=jnp.float32
    )
    fisher = fisher_map(correlation).astype(jnp.bfloat16)
    return running + jnp.dot(fisher, vec_slab, preferred_element_type=jnp.float32)


def by_block(series, regressors, span_ids, nuisance_count, owner_order, vectors):
    grp_count = lax.axis_size("grp")
    rep_count = lax.axis_size("rep")
    rep_index = lax.axis_index("rep")
    frames_loc = series.shape[0]
    frames = frames_loc * grp_count
    own_cols = series.shape[1] // (grp_count * rep_count)
    operators = block_operators(span_ids, frames)
    nuisance = lax.all_gather(regressors, "grp", axis=0, tiled=True)
    masked, lower_factor = nuisance_basis(band_pass(nuisance, operators), nuisance_count)
    quarter = series.reshape(frames_loc, grp_count, rep_count, own_cols)
    quarter = lax.dynamic_slice_in_dim(quarter, rep_index, 1, 2).reshape(
        frames_loc, grp_count, own_cols
    )
    filtered = band_pass(
        lax.all_to_all(quarter, "grp", split_axis=1, concat_axis=0, tiled=True)[:, 0, :].astype(
            jnp.float32
        ),
        operators,
    )
    unit_cols = scale_columns(filtered, masked, lower_factor)
    projected = jnp.zeros((own_cols, vectors.shape[1]), jnp.float32)
    for number in range(BLOCKS):
        piece_in, vec_slab = (
            spread_2(unit_cols, "grp", owner_order[number]),
            spread_2(vectors, "grp", owner_order[number]),
        )
        projected = fold_tile(
            unit_cols, vec_slab, projected, lax.all_gather(piece_in, "rep", axis=1, tiled=True)
        )
    return projected


def solution(mesh):
    local = one_kernel if mesh.shape["grp"] == BLOCKS and mesh.shape["rep"] == 4 else by_block
    placed = (P("grp", None), P("grp", None), P(), P(), P(), P("grp", None))
    return jax.shard_map(
        local, mesh=mesh, in_specs=placed, out_specs=P(("grp", "rep"), None), check_vma=False
    )
```

```python
import functools
import math

import jax
import jax.numpy as jnp
from jax import lax
from jax.experimental import pallas as pl
from jax.experimental.pallas import tpu as pltpu
from jax.sharding import PartitionSpec as P

BLOCKS = 8
MESH = pl.DeviceIdType.MESH
HIGHEST = lax.Precision.HIGHEST

fast_pole = 0.64
slow_pole = 0.955
corr_limit = 0.99
norm_eps = 1e-06


def dot32(a, b, ca, cb):
    return lax.dot_general(
        a, b, (((ca,), (cb,)), ((), ())), precision=HIGHEST, preferred_element_type=jnp.float32
    )


def dot16(a, b, ca, cb):
    return lax.dot_general(
        a, b, (((ca,), (cb,)), ((), ())), preferred_element_type=jnp.float32
    )


def band_matrix(span_row):
    frames = span_row.shape[1]
    across = jnp.broadcast_to(span_row.astype(jnp.float32), (frames, frames))
    down = across.T
    lag = lax.broadcasted_iota(jnp.int32, (frames, frames), 0) - lax.broadcasted_iota(
        jnp.int32, (frames, frames), 1
    )
    steps = jnp.maximum(lag, 0).astype(jnp.float32)
    fast = (1.0 - fast_pole) * jnp.exp(steps * math.log(fast_pole))
    slow = (1.0 - slow_pole) * jnp.exp(steps * math.log(slow_pole))
    return jnp.where((lag >= 0) & (across == down), fast - slow, 0.0)


def spd_inverse(gram):
    size = gram.shape[0]
    lane = lax.broadcasted_iota(jnp.int32, (size, size), 1)
    sub = lax.broadcasted_iota(jnp.int32, (size, size), 0)

    def sweep(k, m):
        on_col, on_row = lane == k, sub == k
        col = jnp.sum(jnp.where(on_col, m, 0.0), axis=1, keepdims=True)
        row = jnp.sum(jnp.where(on_row, m, 0.0), axis=0, keepdims=True)
        pivot = jnp.sum(jnp.where(on_col & on_row, m, 0.0), axis=(0, 1), keepdims=True)
        inv = 1.0 / pivot
        rest = m - col * (row * inv)
        return jnp.where(
            on_row,
            jnp.where(on_col, inv, row * inv),
            jnp.where(on_col, -col * inv, rest),
        )

    return lax.fori_loop(0, size, sweep, gram)


def kernel(
    series, regs, span, count, owner, vectors, out,
    win, rows, nreg, vtb, a_hi, a_lo, unit, unit_rows, parts, other,
    send, reg_r, win_r, vt_r, rows_r, fin_r, loc,
):
    grp, rep = lax.axis_index("grp"), lax.axis_index("rep")
    z, x = grp // 2, grp % 2
    y, c = rep // 2, rep % 2
    groups = lax.axis_size("grp")
    reps = lax.axis_size("rep")
    nz = groups // 2
    frames_loc, gray = series.shape
    slab = gray // groups
    part = 2 * slab
    wide = rows.shape[1]
    quarter = out.shape[1]
    pair = y + c * (nz - 1 - 2 * y)
    home = pair == z
    away = pair != z

    near = z + 1 - 2 * (z % 2)
    far = [nz - 1 - z, lax.rem(z + nz // 2, nz)]
    x_peer = (z * 2 + 1 - x, rep)
    diagonal = (near * 2 + 1 - x, rep)
    direct = [(zz * 2 + x, rep) for zz in [near] + far] + [x_peer, diagonal]
    mates = [lax.rem(rep + d, reps) for d in range(1, reps)]

    barrier = pltpu.get_barrier_semaphore()
    across = [(zz * 2 + 1 - x, rep) for zz in far]
    everyone = direct + across + [(grp, k) for k in mates]
    for peer in everyone:
        pl.semaphore_signal(barrier, inc=1, device_id=peer, device_id_type=MESH)

    sent = []

    def push(src, dst, recv, peer, cond=None):
        copy = pltpu.make_async_remote_copy(
            src_ref=src, dst_ref=dst, send_sem=send.at[len(sent)], recv_sem=recv,
            device_id=peer, device_id_type=MESH,
        )
        if cond is None:
            copy.start()
        else:
            pl.when(cond)(copy.start)
        sent.append((copy, cond))

    def arrive(dst, recv):
        pltpu.make_async_copy(dst, dst, recv).wait()

    def rows_of(s):
        return pl.ds(pl.multiple_of(s * frames_loc, frames_loc), frames_loc)

    part_cols = pl.ds(pl.multiple_of(pair * part, 128), part)
    slab_at = pl.multiple_of(grp * slab - (slab % 128) * x, 128)
    slab_in_part = pl.ds(pl.multiple_of(x * (slab - slab % 128), 128), wide)

    local_win = pltpu.make_async_copy(
        series.at[:, part_cols], win.at[rows_of(grp), :], loc.at[0]
    )
    local_rows = pltpu.make_async_copy(
        series.at[:, pl.ds(slab_at, wide)], rows.at[rows_of(grp), :], loc.at[1]
    )
    local_win.start()
    local_rows.start()
    nreg[grp] = regs[...]
    nvec = vectors.shape[0]

    @pl.when(home)
    def _():
        vtb[x] = vectors[...]

    pl.semaphore_wait(barrier, len(everyone))

    for peer in direct + across:
        push(regs, nreg.at[grp], reg_r.at[grp], peer)
    for peer in direct:
        push(series.at[:, part_cols], win.at[rows_of(grp), :], win_r.at[grp], peer)
    filt = band_matrix(span[...])

    for zz in far:
        s = zz * 2 + x
        arrive(nreg.at[s], reg_r.at[s])
    for s in [near * 2 + x] + [zz * 2 + 1 - x for zz in [z, near] + far]:
        arrive(nreg.at[s], reg_r.at[s])

    kmax = regs.shape[0]
    active = (lax.broadcasted_iota(jnp.int32, (kmax, 1), 0) < count[0]).astype(jnp.float32)
    frames_in = jnp.concatenate([nreg[s] for s in range(groups)], axis=1)
    masked = dot32(frames_in, filt, 1, 1) * active
    diag = (
        lax.broadcasted_iota(jnp.int32, (kmax, kmax), 0)
        == lax.broadcasted_iota(jnp.int32, (kmax, kmax), 1)
    )
    gram = dot32(masked, masked, 1, 1) + jnp.where(diag, 1.0 - active, 0.0)
    inverse = spd_inverse(gram)

    keeps = []

    def landed(s, forward):
        here = win.at[rows_of(s), :]
        arrive(here, win_r.at[s])
        if forward:
            push(here, here, win_r.at[s], x_peer)
        src = win.at[rows_of(s), slab_in_part]
        dst = rows.at[rows_of(s), :]
        for k in mates:
            push(src, dst, rows_r.at[s], (grp, k), home)
        keep = pltpu.make_async_copy(src, dst, loc.at[2 + len(keeps)])
        pl.when(home)(keep.start)
        keeps.append((keep, dst, rows_r.at[s]))

    for zz in far:
        landed(zz * 2 + x, True)
    for peer in direct[:-1]:
        push(vectors, vtb.at[x], vt_r.at[x], peer, home)

    landed(near * 2 + x, False)
    landed(z * 2 + 1 - x, False)
    landed(near * 2 + 1 - x, False)

    fitted = dot32(inverse, dot32(masked, filt, 1, 0), 1, 0)
    clean = filt - dot32(masked, fitted, 0, 0)
    clean = clean - jnp.mean(clean, axis=0, keepdims=True)
    hi = clean.astype(jnp.bfloat16)
    a_hi[...] = hi
    a_lo[...] = (clean - hi.astype(jnp.float32)).astype(jnp.bfloat16)

    pl.when(away)(lambda: arrive(vtb.at[x], vt_r.at[x]))
    push(vtb.at[x], vtb.at[x], vt_r.at[x], x_peer, away)

    for zz in far:
        landed(zz * 2 + 1 - x, False)
    local_win.wait()
    local_rows.wait()

    def normal(block):
        centered = dot16(a_hi[...], block, 1, 0) + dot16(a_lo[...], block, 1, 0)
        power = jnp.mean(centered * centered, axis=0, keepdims=True) + norm_eps
        return centered * (lax.rsqrt(power) * (1.0 / math.sqrt(centered.shape[0])))

    for start in range(0, part, 256):
        cols = slice(start, min(start + 256, part))
        unit[:, cols] = normal(win[:, cols]).astype(jnp.bfloat16)

    arrive(vtb.at[1 - x], vt_r.at[1 - x])
    right = jnp.concatenate([vtb[t] for t in range(2)], axis=1)
    place = lax.broadcasted_iota(jnp.int32, (1, part), 1)
    which = 2 * pair + (place >= slab).astype(jnp.int32)
    times = jnp.zeros((1, part), jnp.float32)
    for b in range(BLOCKS):
        times = times + jnp.where(which == owner[b], 0.5, 0.0)

    for keep, dst, recv in keeps:
        pl.when(away)(functools.partial(arrive, dst, recv))
        pl.when(home)(keep.wait)
    for start in range(0, wide, 256):
        cols = slice(start, start + 256)
        unit_rows[cols, :] = normal(rows[:, cols]).T.astype(jnp.bfloat16)

    for k in mates + [rep]:
        first = pl.multiple_of((slab % 128) * x + quarter * k, 16)
        left = unit_rows[pl.ds(first, quarter), :]
        corr = jnp.clip(dot16(left, unit[...], 1, 0), -corr_limit, corr_limit)
        fisher = ((jnp.log(1.0 + corr) - jnp.log(1.0 - corr)) * times).astype(jnp.bfloat16)
        parts[k] = dot16(right, fisher, 1, 1)
        if k is not rep:
            push(parts.at[k], other.at[rep], fin_r.at[rep], (grp, k))
    total = parts[rep]
    for k in mates:
        arrive(other.at[k], fin_r.at[k])
        total = total + other[k]
    out[...] = total
    for copy, cond in sent:
        if cond is None:
            copy.wait_send()
        else:
            pl.when(cond)(copy.wait_send)


def one_kernel(series, regressors, span_ids, nuisance_count, owner_order, vectors):
    groups, reps = lax.axis_size("grp"), lax.axis_size("rep")
    frames_loc, gray = series.shape
    frames = frames_loc * groups
    slab = gray // groups
    quarter = slab // reps
    wide = -(-slab // 128) * 128
    nvec = vectors.shape[1]
    vm = pl.BlockSpec(memory_space=pltpu.VMEM)
    sm = pl.BlockSpec(memory_space=pltpu.SMEM)
    dma = pltpu.SemaphoreType.DMA
    return pl.pallas_call(
        kernel,
        out_shape=jax.ShapeDtypeStruct((nvec, quarter), jnp.float32),
        in_specs=[pl.BlockSpec(memory_space=pl.ANY), vm, vm, sm, sm, vm],
        out_specs=vm,
        scratch_shapes=[
            pltpu.VMEM((frames, 2 * slab), jnp.bfloat16),
            pltpu.VMEM((frames, wide), jnp.bfloat16),
            pltpu.VMEM((groups, regressors.shape[1], frames_loc), jnp.float32),
            pltpu.VMEM((2, nvec, slab), jnp.bfloat16),
            pltpu.VMEM((frames, frames), jnp.bfloat16),
            pltpu.VMEM((frames, frames), jnp.bfloat16),
            pltpu.VMEM((frames, 2 * slab), jnp.bfloat16),
            pltpu.VMEM((wide, frames), jnp.bfloat16),
            pltpu.VMEM((reps, nvec, quarter), jnp.float32),
            pltpu.VMEM((reps, nvec, quarter), jnp.float32),
            dma((64,)),
            dma((groups,)), dma((groups,)), dma((2,)),
            dma((groups,)), dma((reps,)), dma((16,)),
        ],
        compiler_params=pltpu.CompilerParams(
            collective_id=0, has_side_effects=True, vmem_limit_bytes=60 * 1024 * 1024
        ),
    )(series, regressors.T, span_ids[None, :], nuisance_count, owner_order, vectors.T).T


def spread_2(value, axis, root):
    mine = lax.axis_index(axis) == root
    return lax.psum(jnp.where(mine, value, jnp.zeros_like(value)), axis)


def fisher_map(correlation):
    clipped = jnp.clip(correlation, -corr_limit, corr_limit)
    return 0.5 * jnp.log((1.0 + clipped) / (1.0 - clipped))


def block_operators(span_ids, frames):
    offsets = jnp.arange(128)
    lag_steps = offsets[:, None] - offsets[None, :]
    lag_clip = jnp.maximum(lag_steps, 0).astype(jnp.float32)
    operators = []
    for number in range(frames // 128):
        ids_here = span_ids[number * 128 : (number + 1) * 128]
        joined = (ids_here[:, None] == ids_here[None, :]) & (lag_steps >= 0)
        if number == 0:
            linked = jnp.zeros((128,), jnp.float32)
        else:
            linked = (ids_here == span_ids[number * 128 - 1]).astype(jnp.float32)
        pole_pair = []
        for pole_value in (fast_pole, slow_pole):
            matrix = jnp.where(
                joined, (1.0 - pole_value) * jnp.exp(lag_clip * math.log(pole_value)), 0.0
            )
            carried = linked * jnp.exp((offsets + 1).astype(jnp.float32) * math.log(pole_value))
            pole_pair.append((matrix, carried))
        operators.append(pole_pair)
    return operators


def band_pass(columns_in, operators):
    col_count = columns_in.shape[1]
    states = [jnp.zeros((col_count,), jnp.float32), jnp.zeros((col_count,), jnp.float32)]
    pieces = []
    for number, pole_pair in enumerate(operators):
        segment = columns_in[number * 128 : (number + 1) * 128]
        outputs = []
        for pole_slot in range(2):
            matrix, carried = pole_pair[pole_slot]
            response = (
                jnp.dot(matrix, segment, precision=lax.Precision.HIGHEST)
                + carried[:, None] * states[pole_slot][None, :]
            )
            states[pole_slot] = response[-1]
            outputs.append(response)
        pieces.append(outputs[0] - outputs[1])
    return jnp.concatenate(pieces, axis=0)


def nuisance_basis(filtered_nuisance, nuisance_count):
    active = (jnp.arange(filtered_nuisance.shape[1]) < nuisance_count[0]).astype(jnp.float32)
    masked = filtered_nuisance * active[None, :]
    gram_matrix = jnp.dot(masked.T, masked, precision=lax.Precision.HIGHEST) + jnp.diag(
        1.0 - active
    )
    return (masked, jnp.linalg.cholesky(gram_matrix))


def scale_columns(filtered, masked, lower_factor):
    highest = lax.Precision.HIGHEST
    right_side = jnp.dot(masked.T, filtered, precision=highest)
    halfway = lax.linalg.triangular_solve(lower_factor, right_side, left_side=True, lower=True)
    coefficients = lax.linalg.triangular_solve(
        lower_factor, halfway, left_side=True, lower=True, transpose_a=True
    )
    cleaned = filtered - jnp.dot(masked, coefficients, precision=highest)
    centered = cleaned - jnp.mean(cleaned, axis=0, keepdims=True)
    spread = lax.rsqrt(jnp.mean(centered * centered, axis=0, keepdims=True) + norm_eps)
    return (centered * spread * (1.0 / math.sqrt(centered.shape[0]))).astype(jnp.bfloat16)


def fold_tile(my_cols, vec_slab, running, part_cols):
    correlation = lax.dot_general(
        my_cols, part_cols, (((0,), (0,)), ((), ())), preferred_element_type=jnp.float32
    )
    fisher = fisher_map(correlation).astype(jnp.bfloat16)
    return running + jnp.dot(fisher, vec_slab, preferred_element_type=jnp.float32)


def by_block(series, regressors, span_ids, nuisance_count, owner_order, vectors):
    grp_count = lax.axis_size("grp")
    rep_count = lax.axis_size("rep")
    rep_index = lax.axis_index("rep")
    frames_loc = series.shape[0]
    frames = frames_loc * grp_count
    own_cols = series.shape[1] // (grp_count * rep_count)
    operators = block_operators(span_ids, frames)
    nuisance = lax.all_gather(regressors, "grp", axis=0, tiled=True)
    masked, lower_factor = nuisance_basis(band_pass(nuisance, operators), nuisance_count)
    quarter = series.reshape(frames_loc, grp_count, rep_count, own_cols)
    quarter = lax.dynamic_slice_in_dim(quarter, rep_index, 1, 2).reshape(
        frames_loc, grp_count, own_cols
    )
    filtered = band_pass(
        lax.all_to_all(quarter, "grp", split_axis=1, concat_axis=0, tiled=True)[:, 0, :].astype(
            jnp.float32
        ),
        operators,
    )
    unit_cols = scale_columns(filtered, masked, lower_factor)
    projected = jnp.zeros((own_cols, vectors.shape[1]), jnp.float32)
    for number in range(BLOCKS):
        piece_in, vec_slab = (
            spread_2(unit_cols, "grp", owner_order[number]),
            spread_2(vectors, "grp", owner_order[number]),
        )
        projected = fold_tile(
            unit_cols, vec_slab, projected, lax.all_gather(piece_in, "rep", axis=1, tiled=True)
        )
    return projected


def solution(mesh):
    local = one_kernel if mesh.shape["grp"] == BLOCKS and mesh.shape["rep"] == 4 else by_block
    placed = (P("grp", None), P("grp", None), P(), P(), P(), P("grp", None))
    return jax.shard_map(
        local, mesh=mesh, in_specs=placed, out_specs=P(("grp", "rep"), None), check_vma=False
    )
```
